128 devices in a mesh: row: 8 (over z_hi, y), col: 4 (over z_lo, core), depth: 4 (over x).
Axes of the slice: x: 4, y: 4, z: 4 (z_hi: 2, z_lo: 2; z = z_hi * 2 + z_lo), core: 2. Of those that a mesh axis runs over, the one named last changes fastest.
Arguments:
- tokens: bfloat16 [1024, 14848], P(('row', 'col'), 'depth'), may hold values from -6 to 6
- w_up: bfloat16 [14848, 32768], P('depth', ('row', 'col')), may hold values from -0.046875 to 0.046875
- grad_hidden: bfloat16 [1024, 32768], P('depth', ('row', 'col')), may hold values from -6 to 6
Outputs:
- hidden_act: bfloat16 [1024, 32768], P('depth', ('row', 'col'))
- input_grad: bfloat16 [1024, 14848], P(('row', 'col'), 'depth')
- weight_grad: bfloat16 [14848, 32768], P('depth', ('row', 'col'))
The draws below stay inside these ranges and needn't reach their ends.
All inputs are finite; a program needn't handle non-finite values.
Results may differ from the reference program's by a relative error of at most 0.0049.
Values may be sent and summed in bfloat16 or wider, within the bound.
No kernel may reach another device: no remote copies, remote signals or barrier semaphores. Data moves between devices by JAX's collectives and lax.ppermute only.
A program may use at most 128 MiB of HBM per device.

```python
import jax
import jax.numpy as jnp
from jax import lax

D = 14848
FF = 32768
TOKENS = 1024


def strengthened(entries, own_key, source, target, parts, factor):
    owner, partner = [(jnp.arange(entries.shape[axis_at]) // (entries.shape[axis_at] // parts)).reshape([-1 if axis == axis_at else 1 for axis in range(entries.ndim)]) for axis_at in (source, target)]
    chosen = jax.random.permutation(own_key, parts)[partner]
    strong = (owner == chosen) | (owner == (partner + parts // 2) % parts)
    return jnp.where(strong, factor * entries, entries)


def levels(stream_key, shape, pieces, least, high):
    level = 1.0
    for dim, shards_of in pieces:
        steps = jax.random.uniform(jax.random.fold_in(jax.random.fold_in(stream_key, 6), dim), (shards_of,), jnp.float32, least / len(pieces), high / len(pieces))
        level = level * jnp.repeat(jnp.exp(steps), shape[dim] // shards_of).reshape((-1,) + (1,) * (len(shape) - 1 - dim))
    return level


def scatter_about(rng, shape, width, reach, pieces=(), dtype=jnp.bfloat16):
    result = jax.random.normal(rng, shape, jnp.float32) * width
    if len(pieces) > 0:
        result = levels(rng, shape, pieces, -0.22, 0.18) * result
    return jnp.clip(result, min=-reach, max=reach).astype(dtype)


def bell_draw_with(own_key, extent, width, reach, shards, heavy, held_as=jnp.bfloat16):
    array = width * jax.random.normal(own_key, extent, jnp.float32)
    if shards:
        array = array * levels(own_key, extent, shards, -0.22, 0.18)
    return jnp.clip(strengthened(array, jax.random.fold_in(own_key, 3), *heavy), -reach, reach).astype(held_as)


def setup_inputs(seed: int = 0) -> dict:
    seeds = jax.random.split(jax.random.key(seed), 4)
    return {
        "tokens": bell_draw_with(seeds[0], (TOKENS, D), 1.0, 6.0, ((0, 32), (1, 4)), (1, 0, 32, 2.75)),
        "w_up": scatter_about(seeds[1], (D, FF), D ** -0.5, 0.046875, ((0, 4), (1, 32))),
        "grad_hidden": bell_draw_with(seeds[2], (TOKENS, FF), 1.0, 6.0, ((0, 4), (1, 32)), (1, 0, 32, 2.75)),
    }


root_half = 0.7071067811865476
norm_density = 0.3989422804014327


def gelu_value(values):
    return 0.5 * values * (1.0 + lax.erf(values * root_half))


def gelu_slope(values):
    return 0.5 * (1.0 + lax.erf(values * root_half)) + values * norm_density * jnp.exp(-0.5 * values * values)


def reference(tokens, w_up, grad_hidden):
    pre_act = jnp.dot(tokens, w_up, preferred_element_type=jnp.float32)
    hidden_act = gelu_value(pre_act).astype(jnp.bfloat16)
    grad_pre = (grad_hidden.astype(jnp.float32) * gelu_slope(pre_act)).astype(jnp.bfloat16)
    weight_grad = jnp.dot(tokens.T, grad_pre, preferred_element_type=jnp.float32).astype(jnp.bfloat16)
    input_grad = jnp.dot(grad_pre, w_up.T, preferred_element_type=jnp.float32).astype(jnp.bfloat16)
    return hidden_act, input_grad, weight_grad
```

```python
import jax
import jax.numpy as jnp
from jax import lax
from jax.sharding import PartitionSpec as P

root_half = 0.7071067811865476
norm_density = 0.3989422804014327
PLANE = ("row", "col")
f32, bf16 = jnp.float32, jnp.bfloat16


def spot(z, y, core):
    return ((z // 2) * 4 + y) * 4 + (z % 2) * 2 + core


def plane_pairs(leg, way):
    pairs = []
    for z in range(4):
        for y in range(4):
            for core in range(2):
                on_y = (leg == "first") == (core == 0)
                to = ((z, (y + way) % 4) if on_y else ((z + way) % 4, y)) + (core,)
                pairs.append((spot(z, y, core), spot(*to)))
    return pairs


def move(block, leg, way):
    if leg == "depth":
        return lax.ppermute(block, "depth", [(i, (i + way) % 4) for i in range(4)])
    return lax.ppermute(block, PLANE, plane_pairs(leg, way))


def swap(block):
    return lax.ppermute(
        block,
        PLANE,
        [(spot(z, y, c), spot(z, y, 1 - c)) for z in range(4) for y in range(4) for c in range(2)],
    )


def pick(stack, at):
    return lax.dynamic_index_in_dim(stack, at, 0, keepdims=False)


def gather4(block, leg, at):
    half = block.shape[0] // 2
    below, above = move(block, leg, 1), move(block, leg, -1)
    far_low, far_high = move(below[:half], leg, 1), move(above[half:], leg, -1)
    whole = jnp.zeros((4,) + block.shape, block.dtype)
    for shift, part in ((0, block), (3, below), (1, above)):
        whole = lax.dynamic_update_slice_in_dim(whole, part[None], (at + shift) % 4, 0)
    far = jnp.concatenate([far_low, far_high], 0)
    return lax.dynamic_update_slice_in_dim(whole, far[None], (at + 2) % 4, 0)


def scatter4(stack, leg, at):
    half = stack.shape[1] // 2
    far, up, down = (pick(stack, (at + shift) % 4) for shift in (2, 1, 3))
    low = move(far[:half].astype(bf16), leg, 1)
    high = move(far[half:].astype(bf16), leg, -1)
    up = jnp.concatenate([up[:half] + low.astype(f32), up[half:]], 0).astype(bf16)
    down = jnp.concatenate([down[:half], down[half:] + high.astype(f32)], 0).astype(bf16)
    from_below, from_above = move(up, leg, 1), move(down, leg, -1)
    return pick(stack, at) + from_below.astype(f32) + from_above.astype(f32)


def by_owner(rows):
    one = rows[0].reshape((2, 2, 2, 2) + rows.shape[3:])
    two = rows[1].reshape((2, 2, 2, 2) + rows.shape[3:])
    one = one.transpose(0, 2, 1, 3, 4, 5)
    two = two.transpose(2, 0, 1, 3, 4, 5)
    both = jnp.stack([one, two], 2)
    return both.reshape((4,) + both.shape[2:])


def from_owner(rows):
    both = rows.reshape((2, 2) + rows.shape[1:])
    one = both[:, :, 0].transpose(0, 2, 1, 3, 4, 5)
    two = both[:, :, 1].transpose(1, 2, 0, 3, 4, 5)
    return jnp.stack([one.reshape((4, 4) + one.shape[4:]), two.reshape((4, 4) + two.shape[4:])], 0)


def owner_order(rows):
    split = rows.reshape(2, 2, 2, -1, rows.shape[-1])
    return jnp.stack([split[:, :, 0].transpose(1, 0, 2, 3), split[:, :, 1]], 0)


def token_order(rows):
    both = jnp.stack([rows[0].transpose(1, 0, 2, 3), rows[1]], 2)
    return both.reshape(-1, rows.shape[-1])


def shards(tokens, w_up, grad_hidden):
    row, col, depth = lax.axis_index("row"), lax.axis_index("col"), lax.axis_index("depth")
    z, y, core = (row // 4) * 2 + col // 2, row % 4, col % 2
    first, second = jnp.where(core == 0, y, z), jnp.where(core == 0, z, y)
    share, width = tokens.shape
    hidden = w_up.shape[1]

    own = gather4(gather4(tokens, "first", first), "second", second)
    other = swap(own)
    every = jnp.zeros((2,) + own.shape, own.dtype)
    every = lax.dynamic_update_slice_in_dim(every, own[None], core, 0)
    every = lax.dynamic_update_slice_in_dim(every, other[None], 1 - core, 0)
    flat = every.reshape(-1, width)

    partial_value = jnp.dot(flat, w_up, preferred_element_type=f32)
    owned = by_owner(partial_value.reshape(2, 4, 4, share, hidden))
    pre_act = scatter4(owned.reshape(4, -1, hidden), "depth", depth).reshape(owned.shape[1:])

    edge = lax.erf(pre_act * root_half)
    hidden_act = token_order((0.5 * pre_act * (1.0 + edge)).astype(bf16))
    slope = 0.5 * (1.0 + edge) + pre_act * norm_density * jnp.exp(-0.5 * pre_act * pre_act)
    grad_own = (owner_order(grad_hidden).astype(f32) * slope).astype(bf16)
    grads = gather4(grad_own.reshape(-1, hidden), "depth", depth)
    grads = from_owner(grads.reshape((4,) + grad_own.shape)).reshape(2, -1, hidden)

    def back(rows):
        return lax.dot_general(rows, w_up, (((1,), (1,)), ((), ())), preferred_element_type=f32)

    theirs = swap(back(pick(grads, 1 - core)).astype(bf16))
    ours = (back(pick(grads, core)) + theirs.astype(f32)).reshape(4, -1, width)
    line = scatter4(ours, "second", second).reshape(4, share, width)
    input_grad = scatter4(line, "first", first).astype(bf16)
    weight_grad = lax.dot_general(
        flat, grads.reshape(-1, hidden), (((0,), (0,)), ((), ())), preferred_element_type=f32
    ).astype(bf16)
    return hidden_act, input_grad, weight_grad


def solution(mesh):
    placed = (P(PLANE, "depth"), P("depth", PLANE), P("depth", PLANE))
    return jax.shard_map(
        shards,
        mesh=mesh,
        in_specs=placed,
        out_specs=(P("depth", PLANE), P(PLANE, "depth"), P("depth", PLANE)),
        check_vma=False,
    )
```

```python
import jax
import jax.numpy as jnp
from jax import lax
from jax.sharding import PartitionSpec as P

root_half = 0.7071067811865476
norm_density = 0.3989422804014327
PLANE = ("row", "col")
f32, bf16 = jnp.float32, jnp.bfloat16


def spot(z, y, core):
    return ((z // 2) * 4 + y) * 4 + (z % 2) * 2 + core


def plane_pairs(leg, way):
    pairs = []
    for z in range(4):
        for y in range(4):
            for core in range(2):
                on_y = (leg == "first") == (core == 0)
                to = ((z, (y + way) % 4) if on_y else ((z + way) % 4, y)) + (core,)
                pairs.append((spot(z, y, core), spot(*to)))
    return pairs


def move(block, leg, way):
    if leg == "depth":
        return lax.ppermute(block, "depth", [(i, (i + way) % 4) for i in range(4)])
    return lax.ppermute(block, PLANE, plane_pairs(leg, way))


def swap(block):
    return lax.ppermute(
        block,
        PLANE,
        [(spot(z, y, c), spot(z, y, 1 - c)) for z in range(4) for y in range(4) for c in range(2)],
    )


def pick(stack, at):
    return lax.dynamic_index_in_dim(stack, at, 0, keepdims=False)


def place(stack, part, at):
    return lax.dynamic_update_slice_in_dim(stack, part[None], at % 4, 0)


def gather_near(block, leg, at):
    whole = jnp.zeros((4,) + block.shape, block.dtype)
    for shift in (0, 1, 2, 3):
        part = move(block, leg, shift) if shift else block
        whole = place(whole, part, at + 4 - shift)
    return whole


def scatter_near(stack, leg, at):
    total = pick(stack, at)
    for shift in (2, 1, 3):
        total += move(pick(stack, (at + shift) % 4).astype(bf16), leg, shift).astype(f32)
    return total


def cross(block, step):
    pairs = []
    for col in range(4):
        for x in range(4):
            pairs.append((col * 4 + x, col * 4 + ((x ^ 1) if (step + col) % 2 == 0 else 3 - x)))
    return lax.ppermute(block, ("col", "depth"), pairs)


def partner(at, core, step):
    return jnp.where((step + core) % 2 == 0, at ^ 1, 3 - at)


def halve(stack, at, core):
    near, mate = partner(at, core, 0), partner(at, core, 1)
    away = jnp.stack([pick(stack, near), pick(stack, partner(near, core, 1))], 0)
    got = cross(away.astype(bf16), 0).astype(f32)
    send = (pick(stack, mate) + got[1]).astype(bf16)
    back = cross(send, 1).astype(f32)
    return pick(stack, at) + got[0] + back


def double(block, at, core):
    near, mate = partner(at, core, 0), partner(at, core, 1)
    pair = jnp.stack([block, cross(block, 1)], 0)
    got = cross(pair, 0)
    whole = jnp.zeros((4,) + block.shape, block.dtype)
    for part, index in ((pair[0], at), (pair[1], mate), (got[0], near), (got[1], partner(near, core, 1))):
        whole = place(whole, part, index)
    return whole


def by_owner(rows):
    one = rows[0].reshape((2, 2, 2, 2) + rows.shape[3:])
    two = rows[1].reshape((2, 2, 2, 2) + rows.shape[3:])
    one = one.transpose(0, 2, 1, 3, 4, 5)
    two = two.transpose(2, 0, 1, 3, 4, 5)
    both = jnp.stack([one, two], 2)
    return both.reshape((4,) + both.shape[2:])


def from_owner(rows):
    both = rows.reshape((2, 2) + rows.shape[1:])
    one = both[:, :, 0].transpose(0, 2, 1, 3, 4, 5)
    two = both[:, :, 1].transpose(1, 2, 0, 3, 4, 5)
    return jnp.stack([one.reshape((4, 4) + one.shape[4:]), two.reshape((4, 4) + two.shape[4:])], 0)


def owner_order(rows):
    split = rows.reshape(2, 2, 2, -1, rows.shape[-1])
    return jnp.stack([split[:, :, 0].transpose(1, 0, 2, 3), split[:, :, 1]], 0)


def token_order(rows):
    both = jnp.stack([rows[0].transpose(1, 0, 2, 3), rows[1]], 2)
    return both.reshape(-1, rows.shape[-1])


def shards(tokens, w_up, grad_hidden):
    row, col, depth = lax.axis_index("row"), lax.axis_index("col"), lax.axis_index("depth")
    z, y, core = (row // 4) * 2 + col // 2, row % 4, col % 2
    first, second = jnp.where(core == 0, y, z), jnp.where(core == 0, z, y)
    share, width = tokens.shape
    hidden = w_up.shape[1]

    line = gather_near(tokens, "first", first).reshape(-1, width)
    half = line.shape[0] // 2
    below, above = move(line, "second", 1), move(line, "second", -1)
    beyond = jnp.concatenate(
        [move(below[:half], "second", 1), move(above[half:], "second", -1)], 0
    )
    every = jnp.zeros((2, 4) + line.shape, bf16)
    partial_value = jnp.zeros((2, 4, line.shape[0], hidden), f32)
    for shift, part in ((0, line), (3, below), (1, above), (2, beyond)):
        for side, rows, at in ((core, part, second), (1 - core, swap(part), first)):
            spot_of = (side, (at + shift) % 4, 0, 0)
            product = jnp.dot(rows, w_up, preferred_element_type=f32)
            partial_value = lax.dynamic_update_slice(partial_value, product[None, None], spot_of)
            every = lax.dynamic_update_slice(every, rows[None, None], spot_of)
    flat = every.reshape(-1, width)

    owned = by_owner(partial_value.reshape(2, 4, 4, share, hidden))
    pre_act = halve(owned.reshape(4, -1, hidden), depth, core).reshape(owned.shape[1:])

    edge = lax.erf(pre_act * root_half)
    hidden_act = token_order((0.5 * pre_act * (1.0 + edge)).astype(bf16))
    slope = 0.5 * (1.0 + edge) + pre_act * norm_density * jnp.exp(-0.5 * pre_act * pre_act)
    grad_own = (owner_order(grad_hidden).astype(f32) * slope).astype(bf16)
    grads = double(grad_own.reshape(-1, hidden), depth, core)
    grads = from_owner(grads.reshape((4,) + grad_own.shape)).reshape(2, 4, -1, hidden)

    def back(rows):
        return lax.dot_general(rows, w_up, (((1,), (1,)), ((), ())), preferred_element_type=f32)

    def share_of(shift):
        theirs = back(lax.dynamic_slice(grads, (1 - core, (first + shift) % 4, 0, 0), piece)[0, 0])
        ours = back(lax.dynamic_slice(grads, (core, (second + shift) % 4, 0, 0), piece)[0, 0])
        return ours + swap(theirs.astype(bf16)).astype(f32)

    piece = (1, 1) + grads.shape[2:]
    far = share_of(2).astype(bf16)
    low, high = move(far[:half], "second", 1), move(far[half:], "second", -1)
    up, down = share_of(1), share_of(3)
    up = jnp.concatenate([up[:half] + low.astype(f32), up[half:]], 0).astype(bf16)
    down = jnp.concatenate([down[:half], down[half:] + high.astype(f32)], 0).astype(bf16)
    from_below, from_above = move(up, "second", 1), move(down, "second", -1)
    ours = share_of(0) + from_below.astype(f32) + from_above.astype(f32)
    input_grad = scatter_near(ours.reshape(4, share, width), "first", first).astype(bf16)
    weight_grad = lax.dot_general(
        flat, grads.reshape(-1, hidden), (((0,), (0,)), ((), ())), preferred_element_type=f32
    ).astype(bf16)
    return hidden_act, input_grad, weight_grad


def solution(mesh):
    placed = (P(PLANE, "depth"), P("depth", PLANE), P("depth", PLANE))
    return jax.shard_map(
        shards,
        mesh=mesh,
        in_specs=placed,
        out_specs=(P("depth", PLANE), P(PLANE, "depth"), P("depth", PLANE)),
        check_vma=False,
    )
```

```python
import jax
import jax.numpy as jnp
from jax import lax
from jax.experimental import pallas as pl
from jax.experimental.pallas import tpu as pltpu
from jax.sharding import PartitionSpec as P

root_half = 0.7071067811865476
norm_density = 0.3989422804014327
PLANE = ("row", "col")
f32, bf16 = jnp.float32, jnp.bfloat16


def spot(z, y, core):
    return ((z // 2) * 4 + y) * 4 + (z % 2) * 2 + core


def plane_pairs(leg, way):
    pairs = []
    for z in range(4):
        for y in range(4):
            for core in range(2):
                on_y = (leg == "first") == (core == 0)
                to = ((z, (y + way) % 4) if on_y else ((z + way) % 4, y)) + (core,)
                pairs.append((spot(z, y, core), spot(*to)))
    return pairs


def move(block, leg, way):
    if leg == "depth":
        return lax.ppermute(block, "depth", [(i, (i + way) % 4) for i in range(4)])
    return lax.ppermute(block, PLANE, plane_pairs(leg, way))


def swap(block):
    return lax.ppermute(
        block,
        PLANE,
        [(spot(z, y, c), spot(z, y, 1 - c)) for z in range(4) for y in range(4) for c in range(2)],
    )


def pick(stack, at):
    return lax.dynamic_index_in_dim(stack, at, 0, keepdims=False)


def place(stack, part, at):
    return lax.dynamic_update_slice_in_dim(stack, part[None], at % 4, 0)


def gather_near(block, leg, at):
    whole = jnp.zeros((4,) + block.shape, block.dtype)
    for shift in (0, 1, 2, 3):
        part = move(block, leg, shift) if shift else block
        whole = place(whole, part, at + 4 - shift)
    return whole


def scatter_near(stack, leg, at):
    total = pick(stack, at)
    for shift in (2, 1, 3):
        total += move(pick(stack, (at + shift) % 4).astype(bf16), leg, shift).astype(f32)
    return total


def cross(block, step):
    pairs = []
    for col in range(4):
        for x in range(4):
            pairs.append((col * 4 + x, col * 4 + ((x ^ 1) if (step + col) % 2 == 0 else 3 - x)))
    return lax.ppermute(block, ("col", "depth"), pairs)


def partner(at, core, step):
    return jnp.where((step + core) % 2 == 0, at ^ 1, 3 - at)


def halve_out(stack, at, core):
    near = partner(at, core, 0)
    away = jnp.stack([pick(stack, near), pick(stack, partner(near, core, 1))], 0)
    return away.astype(bf16)


def halve_in(stack, got, at, core):
    got = got.astype(f32)
    send = (pick(stack, partner(at, core, 1)) + got[1]).astype(bf16)
    return pick(stack, at) + got[0] + cross(send, 1).astype(f32)


def gather_ring(block, at):
    half = block.shape[0] // 2
    below, above = move(block, "depth", 1), move(block, "depth", -1)
    far = [move(below[:half], "depth", 1), move(above[half:], "depth", -1)]
    whole = jnp.zeros((4,) + block.shape, block.dtype)
    for shift, part in ((0, block), (3, below), (1, above), (2, jnp.concatenate(far, 0))):
        whole = place(whole, part, at + shift)
    return whole


def by_owner(rows):
    one = rows[0].reshape((2, 2, 2, 2) + rows.shape[3:])
    two = rows[1].reshape((2, 2, 2, 2) + rows.shape[3:])
    one = one.transpose(0, 2, 1, 3, 4, 5)
    two = two.transpose(2, 0, 1, 3, 4, 5)
    both = jnp.stack([one, two], 2)
    return both.reshape((4,) + both.shape[2:])


def from_owner(rows):
    both = rows.reshape((2, 2) + rows.shape[1:])
    one = both[:, :, 0].transpose(0, 2, 1, 3, 4, 5)
    two = both[:, :, 1].transpose(1, 2, 0, 3, 4, 5)
    return jnp.stack([one.reshape((4, 4) + one.shape[4:]), two.reshape((4, 4) + two.shape[4:])], 0)


def owner_order(rows):
    split = rows.reshape(2, 2, 2, -1, rows.shape[-1])
    return jnp.stack([split[:, :, 0].transpose(1, 0, 2, 3), split[:, :, 1]], 0)


def token_order(rows):
    both = jnp.stack([rows[0].transpose(1, 0, 2, 3), rows[1]], 2)
    return both.reshape(-1, rows.shape[-1])


def turn_block(after_ref, block_ref, out_ref):
    out_ref[...] = block_ref[...].T


def turn(matrix, after):
    rows, columns = matrix.shape
    step = 256
    return pl.pallas_call(
        turn_block,
        grid=(columns // step,),
        in_specs=[
            pl.BlockSpec(after.shape, lambda i: (0, 0)),
            pl.BlockSpec((rows, step), lambda i: (0, i)),
        ],
        out_specs=pl.BlockSpec((step, rows), lambda i: (i, 0)),
        out_shape=jax.ShapeDtypeStruct((columns, rows), matrix.dtype),
        compiler_params=pltpu.CompilerParams(vmem_limit_bytes=24 * 2**20),
        cost_estimate=pl.CostEstimate(
            flops=0, bytes_accessed=4 * rows * columns, transcendentals=0
        ),
    )(after, matrix)


def shards(tokens, w_up, grad_hidden):
    row, col, depth = lax.axis_index("row"), lax.axis_index("col"), lax.axis_index("depth")
    z, y, core = (row // 4) * 2 + col // 2, row % 4, col % 2
    first, second = jnp.where(core == 0, y, z), jnp.where(core == 0, z, y)
    share, width = tokens.shape
    hidden = w_up.shape[1]

    line = gather_near(tokens, "first", first).reshape(-1, width)
    half = line.shape[0] // 2
    below, above = move(line, "second", 1), move(line, "second", -1)
    beyond = jnp.concatenate(
        [move(below[:half], "second", 1), move(above[half:], "second", -1)], 0
    )
    every = jnp.zeros((2, 4) + line.shape, bf16)
    partial_value = jnp.zeros((2, 4, line.shape[0], hidden), f32)
    for shift, part in ((0, line), (3, below), (1, above), (2, beyond)):
        if shift == 2:
            partial_value, part = tie(partial_value, part)
        for side, rows, at in ((core, part, second), (1 - core, swap(part), first)):
            spot_of = (side, (at + shift) % 4, 0, 0)
            product = jnp.dot(rows, w_up, preferred_element_type=f32)
            partial_value = lax.dynamic_update_slice(partial_value, product[None, None], spot_of)
            every = lax.dynamic_update_slice(every, rows[None, None], spot_of)
    flat = every.reshape(-1, width)

    owned = by_owner(partial_value.reshape(2, 4, 4, share, hidden))
    shape = owned.shape[1:-1]
    stack = owned.reshape(4, -1, hidden)
    away = halve_out(stack, depth, core)
    got = cross(away, 0)
    turned = turn(w_up, away[0, :16, :128])
    turned, got = tie(turned, got)
    turned_other = swap(turned)
    pre_act = halve_in(stack, got, depth, core).reshape(shape + (hidden,))
    edge = lax.erf(pre_act * root_half)
    hidden_act = token_order((0.5 * pre_act * (1.0 + edge)).astype(bf16))
    slope = 0.5 * (1.0 + edge) + pre_act * norm_density * jnp.exp(-0.5 * pre_act * pre_act)
    grad_own = (owner_order(grad_hidden).astype(f32) * slope).astype(bf16)
    grads = gather_ring(grad_own.reshape(-1, hidden), depth)
    grads = from_owner(grads.reshape((4,) + grad_own.shape)).reshape((2, 4, -1, hidden))
    mine, theirs = pick(grads, core), swap(pick(grads, 1 - core))

    def share_of(mine, theirs, shift):
        at = (second + shift) % 4
        here = jnp.dot(pick(mine, at), turned, preferred_element_type=f32)
        return here + jnp.dot(pick(theirs, at), turned_other, preferred_element_type=f32)

    far = share_of(mine, theirs, 2).astype(bf16)
    far, mine, theirs = tie(far, mine, theirs)
    low, high = move(far[:half], "second", 1), move(far[half:], "second", -1)
    up, down = share_of(mine, theirs, 1), share_of(mine, theirs, 3)
    up = jnp.concatenate([up[:half] + low.astype(f32), up[half:]], 0).astype(bf16)
    down = jnp.concatenate([down[:half], down[half:] + high.astype(f32)], 0).astype(bf16)
    up, down, grads, flat = tie(up, down, grads, flat)
    from_below, from_above = move(up, "second", 1), move(down, "second", -1)
    weight_grad = lax.dot_general(
        flat, grads.reshape(-1, hidden), (((0,), (0,)), ((), ())), preferred_element_type=f32
    ).astype(bf16)
    ours = share_of(mine, theirs, 0)
    weight_grad, ours, from_below, from_above = tie(weight_grad, ours, from_below, from_above)
    ours = ours + from_below.astype(f32) + from_above.astype(f32)
    input_grad = scatter_near(ours.reshape(4, share, width), "first", first).astype(bf16)
    return hidden_act, input_grad, weight_grad


def tie(*values):
    return lax.optimization_barrier(values)


def solution(mesh):
    placed = (P(PLANE, "depth"), P("depth", PLANE), P("depth", PLANE))
    return jax.shard_map(
        shards,
        mesh=mesh,
        in_specs=placed,
        out_specs=(P("depth", PLANE), P(PLANE, "depth"), P("depth", PLANE)),
        check_vma=False,
    )
```

```python
import jax
import jax.numpy as jnp
from jax import lax
from jax.experimental import pallas as pl
from jax.experimental.pallas import tpu as pltpu
from jax.sharding import PartitionSpec as P

root_half = 0.7071067811865476
norm_density = 0.3989422804014327
PLANE = ("row", "col")
f32, bf16 = jnp.float32, jnp.bfloat16


def spot(z, y, core):
    return ((z // 2) * 4 + y) * 4 + (z % 2) * 2 + core


def plane_pairs(leg, way):
    pairs = []
    for z in range(4):
        for y in range(4):
            for core in range(2):
                on_y = (leg == "first") == (core == 0)
                to = ((z, (y + way) % 4) if on_y else ((z + way) % 4, y)) + (core,)
                pairs.append((spot(z, y, core), spot(*to)))
    return pairs


def move(block, leg, way):
    if leg == "depth":
        return lax.ppermute(block, "depth", [(i, (i + way) % 4) for i in range(4)])
    return lax.ppermute(block, PLANE, plane_pairs(leg, way))


def swap(block):
    return lax.ppermute(
        block,
        PLANE,
        [(spot(z, y, c), spot(z, y, 1 - c)) for z in range(4) for y in range(4) for c in range(2)],
    )


def pick(stack, at):
    return lax.dynamic_index_in_dim(stack, at, 0, keepdims=False)


def place(stack, part, at):
    return lax.dynamic_update_slice_in_dim(stack, part[None], at % 4, 0)


def gather_near(block, leg, at):
    whole = jnp.zeros((4,) + block.shape, block.dtype)
    for shift in (0, 1, 2, 3):
        part = move(block, leg, shift) if shift else block
        whole = place(whole, part, at + 4 - shift)
    return whole


def scatter_near(stack, leg, at):
    total = pick(stack, at)
    for shift in (2, 1, 3):
        total += move(pick(stack, (at + shift) % 4).astype(bf16), leg, shift).astype(f32)
    return total


def cross(block, step):
    pairs = []
    for col in range(4):
        for x in range(4):
            pairs.append((col * 4 + x, col * 4 + ((x ^ 1) if (step + col) % 2 == 0 else 3 - x)))
    return lax.ppermute(block, ("col", "depth"), pairs)


def partner(at, core, step):
    return jnp.where((step + core) % 2 == 0, at ^ 1, 3 - at)


def halve_out(stack, at, core):
    near = partner(at, core, 0)
    away = jnp.stack([pick(stack, near), pick(stack, partner(near, core, 1))], 0)
    return away.astype(bf16)


def halve_in(stack, got, at, core):
    got = got.astype(f32)
    send = (pick(stack, partner(at, core, 1)) + got[1]).astype(bf16)
    return pick(stack, at) + got[0] + cross(send, 1).astype(f32)


def gather_ring(block, at):
    half = block.shape[0] // 2
    below, above = move(block, "depth", 1), move(block, "depth", -1)
    far = [move(below[:half], "depth", 1), move(above[half:], "depth", -1)]
    whole = jnp.zeros((4,) + block.shape, block.dtype)
    for shift, part in ((0, block), (3, below), (1, above), (2, jnp.concatenate(far, 0))):
        whole = place(whole, part, at + shift)
    return whole


def by_owner(rows):
    one = rows[0].reshape((2, 2, 2, 2) + rows.shape[3:])
    two = rows[1].reshape((2, 2, 2, 2) + rows.shape[3:])
    one = one.transpose(0, 2, 1, 3, 4, 5)
    two = two.transpose(2, 0, 1, 3, 4, 5)
    both = jnp.stack([one, two], 2)
    return both.reshape((4,) + both.shape[2:])


def from_owner(rows):
    both = rows.reshape((2, 2) + rows.shape[1:])
    one = both[:, :, 0].transpose(0, 2, 1, 3, 4, 5)
    two = both[:, :, 1].transpose(1, 2, 0, 3, 4, 5)
    return jnp.stack([one.reshape((4, 4) + one.shape[4:]), two.reshape((4, 4) + two.shape[4:])], 0)


def owner_order(rows):
    split = rows.reshape(2, 2, 2, -1, rows.shape[-1])
    return jnp.stack([split[:, :, 0].transpose(1, 0, 2, 3), split[:, :, 1]], 0)


def token_order(rows):
    both = jnp.stack([rows[0].transpose(1, 0, 2, 3), rows[1]], 2)
    return both.reshape(-1, rows.shape[-1])


def turn_block(after_ref, *refs):
    blocks, (out_ref, mark_ref) = refs[:-2], refs[-2:]
    for i, block in enumerate(blocks):

        @pl.when(pl.program_id(0) == i)
        def _(block=block):
            out_ref[...] = block[...].T

    mark_ref[...] = after_ref[...]


def turn(matrices, after):
    rows, columns = matrices[0].shape
    step = 256
    count = columns // step

    def at(i):
        return lambda m, j: (0, jnp.where(m == i, j, jnp.where(m < i, 0, count - 1)))

    return pl.pallas_call(
        turn_block,
        grid=(len(matrices), count),
        in_specs=[pl.BlockSpec(after.shape, lambda m, j: (0, 0))]
        + [pl.BlockSpec((rows, step), at(i)) for i in range(len(matrices))],
        out_specs=[
            pl.BlockSpec((step, rows), lambda m, j: (m * count + j, 0)),
            pl.BlockSpec(after.shape, lambda m, j: (0, 0)),
        ],
        out_shape=[
            jax.ShapeDtypeStruct((len(matrices) * columns, rows), matrices[0].dtype),
            jax.ShapeDtypeStruct(after.shape, after.dtype),
        ],
        compiler_params=pltpu.CompilerParams(vmem_limit_bytes=24 * 2**20),
        cost_estimate=pl.CostEstimate(
            flops=0, bytes_accessed=4 * len(matrices) * rows * columns, transcendentals=0
        ),
    )(after, *matrices)


def shards(tokens, w_up, grad_hidden):
    row, col, depth = lax.axis_index("row"), lax.axis_index("col"), lax.axis_index("depth")
    z, y, core = (row // 4) * 2 + col // 2, row % 4, col % 2
    first, second = jnp.where(core == 0, y, z), jnp.where(core == 0, z, y)
    share, width = tokens.shape
    hidden = w_up.shape[1]

    w_other = swap(w_up)
    line = gather_near(tokens, "first", first).reshape(-1, width)
    half = line.shape[0] // 2
    below, above = move(line, "second", 1), move(line, "second", -1)
    beyond = jnp.concatenate(
        [move(below[:half], "second", 1), move(above[half:], "second", -1)], 0
    )
    every = jnp.zeros((2, 4) + line.shape, bf16)
    partial_value = jnp.zeros((2, 4, line.shape[0], hidden), f32)
    for shift, part in ((0, line), (3, below), (1, above), (2, beyond)):
        for side, rows, at in ((core, part, second), (1 - core, swap(part), first)):
            spot_of = (side, (at + shift) % 4, 0, 0)
            product = jnp.dot(rows, w_up, preferred_element_type=f32)
            partial_value = lax.dynamic_update_slice(partial_value, product[None, None], spot_of)
            every = lax.dynamic_update_slice(every, rows[None, None], spot_of)
    owned = by_owner(partial_value.reshape(2, 4, 4, share, hidden))
    shape = owned.shape[1:-1]
    stack = owned.reshape(4, -1, hidden)
    away = halve_out(stack, depth, core)
    got = cross(away, 0)
    turned, mark = turn((w_up, w_other), away[0, :16, :128])
    turned, got = tie(turned, got)
    pre_act = halve_in(stack, got, depth, core).reshape(shape + (hidden,))
    edge = lax.erf(pre_act * root_half)
    hidden_act = token_order((0.5 * pre_act * (1.0 + edge)).astype(bf16))
    slope = 0.5 * (1.0 + edge) + pre_act * norm_density * jnp.exp(-0.5 * pre_act * pre_act)
    grad_own = (owner_order(grad_hidden).astype(f32) * slope).astype(bf16)
    grads = gather_ring(grad_own.reshape(-1, hidden), depth)
    grads = from_owner(grads.reshape((4,) + grad_own.shape)).reshape((2, 4, -1, hidden))
    mine, theirs = pick(grads, core), swap(pick(grads, 1 - core))

    def share_of(mine, theirs, shift):
        at = (second + shift) % 4
        return jnp.dot(
            jnp.concatenate([pick(mine, at), pick(theirs, at)], 1),
            turned,
            preferred_element_type=f32,
        )

    far = share_of(mine, theirs, 2).astype(bf16)
    far, mine, theirs = tie(far, mine, theirs)
    low, high = move(far[:half], "second", 1), move(far[half:], "second", -1)
    up, down = share_of(mine, theirs, 1), share_of(mine, theirs, 3)
    up = jnp.concatenate([up[:half] + low.astype(f32), up[half:]], 0).astype(bf16)
    down = jnp.concatenate([down[:half], down[half:] + high.astype(f32)], 0).astype(bf16)
    flat = every.reshape(-1, width)
    up, down, grads, flat = tie(up, down, grads, flat)
    from_below, from_above = move(up, "second", 1), move(down, "second", -1)
    weight_grad = lax.dot_general(
        flat, grads.reshape(-1, hidden), (((0,), (0,)), ((), ())), preferred_element_type=f32
    ).astype(bf16)
    ours = share_of(mine, theirs, 0)
    weight_grad, ours, from_below, from_above = tie(weight_grad, ours, from_below, from_above)
    ours = ours + from_below.astype(f32) + from_above.astype(f32)
    input_grad = scatter_near(ours.reshape(4, share, width), "first", first).astype(bf16)
    return hidden_act, input_grad, weight_grad


def tie(*values):
    return lax.optimization_barrier(values)


def solution(mesh):
    placed = (P(PLANE, "depth"), P("depth", PLANE), P("depth", PLANE))
    return jax.shard_map(
        shards,
        mesh=mesh,
        in_specs=placed,
        out_specs=(P("depth", PLANE), P(PLANE, "depth"), P("depth", PLANE)),
        check_vma=False,
    )
```

```python
import jax
import jax.numpy as jnp
from jax import lax
from jax.experimental import pallas as pl
from jax.experimental.pallas import tpu as pltpu
from jax.sharding import PartitionSpec as P

root_half = 0.7071067811865476
norm_density = 0.3989422804014327
PLANE = ("row", "col")
f32, bf16 = jnp.float32, jnp.bfloat16


def spot(z, y, core):
    return ((z // 2) * 4 + y) * 4 + (z % 2) * 2 + core


def plane_pairs(leg, way):
    pairs = []
    for z in range(4):
        for y in range(4):
            for core in range(2):
                on_y = (leg == "first") == (core == 0)
                to = ((z, (y + way) % 4) if on_y else ((z + way) % 4, y)) + (core,)
                pairs.append((spot(z, y, core), spot(*to)))
    return pairs


def move(block, leg, way):
    if leg == "depth":
        return lax.ppermute(block, "depth", [(i, (i + way) % 4) for i in range(4)])
    return lax.ppermute(block, PLANE, plane_pairs(leg, way))


def swap(block):
    return lax.ppermute(
        block,
        PLANE,
        [(spot(z, y, c), spot(z, y, 1 - c)) for z in range(4) for y in range(4) for c in range(2)],
    )


def pick(stack, at):
    return lax.dynamic_index_in_dim(stack, at, 0, keepdims=False)


def place(stack, part, at):
    return lax.dynamic_update_slice_in_dim(stack, part[None], at % 4, 0)


def gather_near(block, leg, at):
    whole = jnp.zeros((4,) + block.shape, block.dtype)
    for shift in (0, 1, 2, 3):
        part = move(block, leg, shift) if shift else block
        whole = place(whole, part, at + 4 - shift)
    return whole


def scatter_near(stack, leg, at):
    total = pick(stack, at)
    for shift in (2, 1, 3):
        total += move(pick(stack, (at + shift) % 4).astype(bf16), leg, shift).astype(f32)
    return total


def cross(block, step):
    pairs = []
    for col in range(4):
        for x in range(4):
            pairs.append((col * 4 + x, col * 4 + ((x ^ 1) if (step + col) % 2 == 0 else 3 - x)))
    return lax.ppermute(block, ("col", "depth"), pairs)


def partner(at, core, step):
    return jnp.where((step + core) % 2 == 0, at ^ 1, 3 - at)


def turn_block(after_ref, *refs):
    blocks, out_ref = refs[:-1], refs[-1]
    for i, block in enumerate(blocks):

        @pl.when(pl.program_id(0) == i)
        def _(block=block):
            out_ref[...] = block[...].T


def turn(matrices, after):
    rows, columns = matrices[0].shape
    step = 256
    count = columns // step

    def at(i):
        return lambda m, j: (0, jnp.where(m == i, j, jnp.where(m < i, 0, count - 1)))

    return pl.pallas_call(
        turn_block,
        grid=(len(matrices), count),
        in_specs=[pl.BlockSpec(after.shape, lambda m, j: (0, 0))]
        + [pl.BlockSpec((rows, step), at(i)) for i in range(len(matrices))],
        out_specs=pl.BlockSpec((step, rows), lambda m, j: (m * count + j, 0)),
        out_shape=jax.ShapeDtypeStruct((len(matrices) * columns, rows), matrices[0].dtype),
        compiler_params=pltpu.CompilerParams(vmem_limit_bytes=24 * 2**20),
        cost_estimate=pl.CostEstimate(
            flops=0, bytes_accessed=4 * len(matrices) * rows * columns, transcendentals=0
        ),
    )(after, *matrices)


def hold_block(after_ref, block_ref, out_ref):
    out_ref[...] = block_ref[...]


def hold(matrix, after):
    rows, columns = matrix.shape
    step = 256
    return pl.pallas_call(
        hold_block,
        grid=(columns // step,),
        in_specs=[
            pl.BlockSpec(after.shape, lambda i: (0, 0)),
            pl.BlockSpec((rows, step), lambda i: (0, i)),
        ],
        out_specs=pl.BlockSpec((rows, step), lambda i: (0, i)),
        out_shape=jax.ShapeDtypeStruct(matrix.shape, matrix.dtype),
        compiler_params=pltpu.CompilerParams(vmem_limit_bytes=24 * 2**20),
        cost_estimate=pl.CostEstimate(
            flops=0, bytes_accessed=4 * rows * columns, transcendentals=0
        ),
    )(after, matrix)


def shards(tokens, w_up, grad_hidden):
    row, col, depth = lax.axis_index("row"), lax.axis_index("col"), lax.axis_index("depth")
    z, y, core = (row // 4) * 2 + col // 2, row % 4, col % 2
    first, second = jnp.where(core == 0, y, z), jnp.where(core == 0, z, y)
    share, width = tokens.shape
    hidden = w_up.shape[1]

    def slot(at):
        return jnp.where(core == 0, at % 4, (at % 2) * 2 + (at % 4) // 2)

    def side_order(rows):
        return jnp.where(core == 0, rows.swapaxes(0, 1), rows)

    w_other = swap(w_up)
    cotangent = grad_hidden.reshape(2, 2, 2, share, hidden)
    cotangent_other = swap(lax.dynamic_index_in_dim(cotangent, 1 - core, 2, keepdims=False))
    cotangent = lax.dynamic_index_in_dim(cotangent, core, 2, keepdims=False)

    line = gather_near(tokens, "first", first).reshape(-1, width)
    count = line.shape[0]
    half = count // 2
    below, above = move(line, "second", 1), move(line, "second", -1)
    held = hold(w_other, line[:16, :128])
    held, below, above = tie(held, below, above)
    beyond = jnp.concatenate(
        [move(below[:half], "second", 1), move(above[half:], "second", -1)], 0
    )
    every = jnp.zeros((2, 4) + line.shape, bf16)
    sums = [jnp.zeros((4, count, hidden), f32) for _ in range(2)]
    for shift, part in ((0, line), (3, below), (1, above), (2, beyond)):
        every = lax.dynamic_update_slice(every, part[None, None], (0, (second + shift) % 4, 0, 0))
        every = lax.dynamic_update_slice(
            every, swap(part)[None, None], (1, (first + shift) % 4, 0, 0)
        )
        for i, weight in enumerate((w_up, held)):
            product = jnp.dot(part, weight, preferred_element_type=f32)
            sums[i] = place(sums[i], product, second + shift)

    def split(total):
        rows = total.reshape(2, 2, 2, 2, share, hidden).transpose(0, 2, 1, 3, 4, 5)
        return rows.reshape(4, count, hidden)

    stack = jnp.concatenate([split(total) for total in sums], -1)
    near, mate = partner(depth, core, 0), partner(depth, core, 1)
    near_mate = partner(near, core, 1)
    away = jnp.stack([pick(stack, slot(near)), pick(stack, slot(near_mate))], 0).astype(bf16)
    got = cross(away, 0)
    turned = turn((w_up, held), away[0, :16, :128])
    turned, got = tie(turned, got)
    send = (pick(stack, slot(mate)) + got[1].astype(f32)).astype(bf16)
    pre_act = pick(stack, slot(depth)) + got[0].astype(f32) + cross(send, 1).astype(f32)

    edge = lax.erf(pre_act * root_half)
    act = (0.5 * pre_act * (1.0 + edge)).astype(bf16).reshape(2, 2, share, 2 * hidden)
    slope = 0.5 * (1.0 + edge) + pre_act * norm_density * jnp.exp(-0.5 * pre_act * pre_act)
    cotangent = side_order(jnp.concatenate([cotangent, cotangent_other], -1))
    grad_own = (cotangent.reshape(pre_act.shape).astype(f32) * slope).astype(bf16)

    lower, upper = move(grad_own, "depth", 1), move(grad_own, "depth", -1)
    middle = count // 2
    opposite = jnp.concatenate(
        [move(lower[:middle], "depth", 1), move(upper[middle:], "depth", -1)], 0
    )
    grads = jnp.zeros((4,) + grad_own.shape, bf16)
    for shift, part in ((0, grad_own), (3, lower), (1, upper), (2, opposite)):
        grads = place(grads, part, slot(depth + shift))
    grads = grads.reshape(2, 2, 2, 2 * share, 2 * hidden)

    def piece_of(grads, shift):
        at = (second + shift) % 4
        return lax.dynamic_slice(
            grads, (at // 2, 0, at % 2, 0, 0), (1, 2, 1) + grads.shape[3:]
        ).reshape(count, 2 * hidden)

    far = jnp.dot(piece_of(grads, 2), turned, preferred_element_type=f32).astype(bf16)
    far, grads = tie(far, grads)
    low, high = move(far[:half], "second", 1), move(far[half:], "second", -1)
    rest = jnp.concatenate([piece_of(grads, shift) for shift in (1, 3, 0)], 0)
    rest = jnp.dot(rest, turned, preferred_element_type=f32)
    up, down, ours = rest[:count], rest[count : 2 * count], rest[2 * count :]
    up = jnp.concatenate([up[:half] + low.astype(f32), up[half:]], 0).astype(bf16)
    down = jnp.concatenate([down[:half], down[half:] + high.astype(f32)], 0).astype(bf16)

    order = grads.transpose(0, 2, 1, 3, 4).reshape(16 * share, 2 * hidden)
    beside = jnp.concatenate([order[:, :hidden], swap(order[:, hidden:])], 0)
    flat = every.reshape(-1, width)
    up, down, beside, flat = tie(up, down, beside, flat)
    from_below, from_above = move(up, "second", 1), move(down, "second", -1)
    weight_grad = lax.dot_general(
        flat, beside, (((0,), (0,)), ((), ())), preferred_element_type=f32
    ).astype(bf16)
    weight_grad, ours, from_below, from_above = tie(weight_grad, ours, from_below, from_above)
    ours = ours + from_below.astype(f32) + from_above.astype(f32)
    input_grad = scatter_near(ours.reshape(4, share, width), "first", first).astype(bf16)

    act_own, act_other = side_order(act[..., :hidden]), swap(side_order(act[..., hidden:]))
    hidden_act = jnp.stack(
        [jnp.where(core == 0, act_own, act_other), jnp.where(core == 0, act_other, act_own)], 2
    )
    return hidden_act.reshape(-1, hidden), input_grad, weight_grad


def tie(*values):
    return lax.optimization_barrier(values)


def solution(mesh):
    placed = (P(PLANE, "depth"), P("depth", PLANE), P("depth", PLANE))
    return jax.shard_map(
        shards,
        mesh=mesh,
        in_specs=placed,
        out_specs=(P("depth", PLANE), P(PLANE, "depth"), P("depth", PLANE)),
        check_vma=False,
    )
```

```python
import jax
import jax.numpy as jnp
from jax import lax
from jax.experimental import pallas as pl
from jax.experimental.pallas import tpu as pltpu
from jax.sharding import PartitionSpec as P

root_half = 0.7071067811865476
norm_density = 0.3989422804014327
PLANE = ("row", "col")
f32, bf16 = jnp.float32, jnp.bfloat16


def spot(z, y, core):
    return ((z // 2) * 4 + y) * 4 + (z % 2) * 2 + core


def plane_pairs(leg, way):
    pairs = []
    for z in range(4):
        for y in range(4):
            for core in range(2):
                on_y = (leg == "first") == (core == 0)
                to = ((z, (y + way) % 4) if on_y else ((z + way) % 4, y)) + (core,)
                pairs.append((spot(z, y, core), spot(*to)))
    return pairs


def move(block, leg, way):
    if leg == "depth":
        return lax.ppermute(block, "depth", [(i, (i + way) % 4) for i in range(4)])
    return lax.ppermute(block, PLANE, plane_pairs(leg, way))


def swap(block):
    return lax.ppermute(
        block,
        PLANE,
        [(spot(z, y, c), spot(z, y, 1 - c)) for z in range(4) for y in range(4) for c in range(2)],
    )


def pick(stack, at):
    return lax.dynamic_index_in_dim(stack, at, 0, keepdims=False)


def place(stack, part, at):
    return lax.dynamic_update_slice_in_dim(stack, part[None], at % 4, 0)


def gather_near(block, leg, at):
    whole = jnp.zeros((4,) + block.shape, block.dtype)
    for shift in (0, 1, 2, 3):
        part = move(block, leg, shift) if shift else block
        whole = place(whole, part, at + 4 - shift)
    return whole


def scatter_near(stack, leg, at):
    total = pick(stack, at)
    for shift in (2, 1, 3):
        total += move(pick(stack, (at + shift) % 4).astype(bf16), leg, shift).astype(f32)
    return total


def cross(block, step):
    pairs = []
    for col in range(4):
        for x in range(4):
            pairs.append((col * 4 + x, col * 4 + ((x ^ 1) if (step + col) % 2 == 0 else 3 - x)))
    return lax.ppermute(block, ("col", "depth"), pairs)


def partner(at, core, step):
    return jnp.where((step + core) % 2 == 0, at ^ 1, 3 - at)


def turn_block(after_ref, *refs):
    blocks, out_ref = refs[:-1], refs[-1]
    for i, block in enumerate(blocks):

        @pl.when(pl.program_id(0) == i)
        def _(block=block):
            out_ref[...] = block[...].T


def turn(matrices, after):
    rows, columns = matrices[0].shape
    step = 256
    count = columns // step

    def at(i):
        return lambda m, j: (0, jnp.where(m == i, j, jnp.where(m < i, 0, count - 1)))

    return pl.pallas_call(
        turn_block,
        grid=(len(matrices), count),
        in_specs=[pl.BlockSpec(after.shape, lambda m, j: (0, 0))]
        + [pl.BlockSpec((rows, step), at(i)) for i in range(len(matrices))],
        out_specs=pl.BlockSpec((step, rows), lambda m, j: (m * count + j, 0)),
        out_shape=jax.ShapeDtypeStruct((len(matrices) * columns, rows), matrices[0].dtype),
        compiler_params=pltpu.CompilerParams(vmem_limit_bytes=24 * 2**20),
        cost_estimate=pl.CostEstimate(
            flops=0, bytes_accessed=4 * len(matrices) * rows * columns, transcendentals=0
        ),
    )(after, *matrices)


def hold_block(after_ref, block_ref, out_ref):
    out_ref[...] = block_ref[...]


def hold(matrix, after):
    rows, columns = matrix.shape
    step = 256
    return pl.pallas_call(
        hold_block,
        grid=(columns // step,),
        in_specs=[
            pl.BlockSpec(after.shape, lambda i: (0, 0)),
            pl.BlockSpec((rows, step), lambda i: (0, i)),
        ],
        out_specs=pl.BlockSpec((rows, step), lambda i: (0, i)),
        out_shape=jax.ShapeDtypeStruct(matrix.shape, matrix.dtype),
        compiler_params=pltpu.CompilerParams(vmem_limit_bytes=24 * 2**20),
        cost_estimate=pl.CostEstimate(
            flops=0, bytes_accessed=4 * rows * columns, transcendentals=0
        ),
    )(after, matrix)


def shards(tokens, w_up, grad_hidden):
    row, col, depth = lax.axis_index("row"), lax.axis_index("col"), lax.axis_index("depth")
    z, y, core = (row // 4) * 2 + col // 2, row % 4, col % 2
    first, second = jnp.where(core == 0, y, z), jnp.where(core == 0, z, y)
    share, width = tokens.shape
    hidden = w_up.shape[1]

    def slot(at):
        return jnp.where(core == 0, at % 4, (at % 2) * 2 + (at % 4) // 2)

    def side_order(rows):
        return jnp.where(core == 0, rows.swapaxes(0, 1), rows)

    w_other = swap(w_up)
    cotangent = grad_hidden.reshape(2, 2, 2, share, hidden)
    cotangent_other = swap(lax.dynamic_index_in_dim(cotangent, 1 - core, 2, keepdims=False))
    cotangent = lax.dynamic_index_in_dim(cotangent, core, 2, keepdims=False)

    line = gather_near(tokens, "first", first).reshape(-1, width)
    count = line.shape[0]
    half = count // 2
    below, above = move(line, "second", 1), move(line, "second", -1)
    held = hold(w_other, line[:16, :128])
    held, below, above = tie(held, below, above)
    beyond = jnp.concatenate(
        [move(below[:half], "second", 1), move(above[half:], "second", -1)], 0
    )
    every = jnp.zeros((2, 4) + line.shape, bf16)
    sums = [jnp.zeros((4, count, hidden), f32) for _ in range(2)]
    for shift, part in ((0, line), (3, below), (1, above), (2, beyond)):
        every = lax.dynamic_update_slice(every, part[None, None], (0, (second + shift) % 4, 0, 0))
        every = lax.dynamic_update_slice(
            every, swap(part)[None, None], (1, (first + shift) % 4, 0, 0)
        )
        for i, weight in enumerate((w_up, held)):
            product = jnp.dot(part, weight, preferred_element_type=f32)
            sums[i] = place(sums[i], product, second + shift)

    def split(total):
        rows = total.reshape(2, 2, 2, 2, share, hidden).transpose(0, 2, 1, 3, 4, 5)
        return rows.reshape(4, count, hidden)

    stack = jnp.concatenate([split(total) for total in sums], -1)
    near, mate = partner(depth, core, 0), partner(depth, core, 1)
    near_mate = partner(near, core, 1)
    away = jnp.stack([pick(stack, slot(near)), pick(stack, slot(near_mate))], 0).astype(bf16)
    got = cross(away, 0)
    send = (pick(stack, slot(mate)) + got[1].astype(f32)).astype(bf16)
    pre_act = pick(stack, slot(depth)) + got[0].astype(f32) + cross(send, 1).astype(f32)

    edge = lax.erf(pre_act * root_half)
    act = (0.5 * pre_act * (1.0 + edge)).astype(bf16).reshape(2, 2, share, 2 * hidden)
    slope = 0.5 * (1.0 + edge) + pre_act * norm_density * jnp.exp(-0.5 * pre_act * pre_act)
    cotangent = side_order(jnp.concatenate([cotangent, cotangent_other], -1))
    grad_own = (cotangent.reshape(pre_act.shape).astype(f32) * slope).astype(bf16)

    lower, upper = move(grad_own, "depth", 1), move(grad_own, "depth", -1)
    turned = turn((w_up, held), grad_own[:16, :128])
    turned, lower, upper = tie(turned, lower, upper)
    middle = count // 2
    opposite = jnp.concatenate(
        [move(lower[:middle], "depth", 1), move(upper[middle:], "depth", -1)], 0
    )
    grads = jnp.zeros((4,) + grad_own.shape, bf16)
    for shift, part in ((0, grad_own), (3, lower), (1, upper), (2, opposite)):
        grads = place(grads, part, slot(depth + shift))
    grads = grads.reshape(2, 2, 2, 2 * share, 2 * hidden)

    def piece_of(grads, shift):
        at = (second + shift) % 4
        return lax.dynamic_slice(
            grads, (at // 2, 0, at % 2, 0, 0), (1, 2, 1) + grads.shape[3:]
        ).reshape(count, 2 * hidden)

    far = jnp.dot(piece_of(grads, 2), turned, preferred_element_type=f32).astype(bf16)
    far, grads = tie(far, grads)
    low, high = move(far[:half], "second", 1), move(far[half:], "second", -1)
    rest = jnp.concatenate([piece_of(grads, shift) for shift in (1, 3, 0)], 0)
    rest = jnp.dot(rest, turned, preferred_element_type=f32)
    up, down, ours = rest[:count], rest[count : 2 * count], rest[2 * count :]
    up = jnp.concatenate([up[:half] + low.astype(f32), up[half:]], 0).astype(bf16)
    down = jnp.concatenate([down[:half], down[half:] + high.astype(f32)], 0).astype(bf16)

    order = grads.transpose(0, 2, 1, 3, 4).reshape(16 * share, 2 * hidden)
    beside = jnp.concatenate([order[:, :hidden], swap(order[:, hidden:])], 0)
    flat = every.reshape(-1, width)
    up, down, beside, flat = tie(up, down, beside, flat)
    from_below, from_above = move(up, "second", 1), move(down, "second", -1)
    weight_grad = lax.dot_general(
        flat, beside, (((0,), (0,)), ((), ())), preferred_element_type=f32
    ).astype(bf16)
    weight_grad, ours, from_below, from_above = tie(weight_grad, ours, from_below, from_above)
    ours = ours + from_below.astype(f32) + from_above.astype(f32)
    input_grad = scatter_near(ours.reshape(4, share, width), "first", first).astype(bf16)

    act_own, act_other = side_order(act[..., :hidden]), swap(side_order(act[..., hidden:]))
    hidden_act = jnp.stack(
        [jnp.where(core == 0, act_own, act_other), jnp.where(core == 0, act_other, act_own)], 2
    )
    return hidden_act.reshape(-1, hidden), input_grad, weight_grad


def tie(*values):
    return lax.optimization_barrier(values)


def solution(mesh):
    placed = (P(PLANE, "depth"), P("depth", PLANE), P("depth", PLANE))
    return jax.shard_map(
        shards,
        mesh=mesh,
        in_specs=placed,
        out_specs=(P("depth", PLANE), P(PLANE, "depth"), P("depth", PLANE)),
        check_vma=False,
    )
```

```python
import jax
import jax.numpy as jnp
from jax import lax
from jax.experimental import pallas as pl
from jax.experimental.pallas import tpu as pltpu
from jax.sharding import PartitionSpec as P

root_half = 0.7071067811865476
norm_density = 0.3989422804014327
PLANE = ("row", "col")
f32, bf16 = jnp.float32, jnp.bfloat16


def spot(z, y, core):
    return ((z // 2) * 4 + y) * 4 + (z % 2) * 2 + core


def plane_pairs(leg, way):
    pairs = []
    for z in range(4):
        for y in range(4):
            for core in range(2):
                on_y = (leg == "first") == (core == 0)
                to = ((z, (y + way) % 4) if on_y else ((z + way) % 4, y)) + (core,)
                pairs.append((spot(z, y, core), spot(*to)))
    return pairs


def move(block, leg, way):
    if leg == "depth":
        return lax.ppermute(block, "depth", [(i, (i + way) % 4) for i in range(4)])
    return lax.ppermute(block, PLANE, plane_pairs(leg, way))


def swap(block):
    return lax.ppermute(
        block,
        PLANE,
        [(spot(z, y, c), spot(z, y, 1 - c)) for z in range(4) for y in range(4) for c in range(2)],
    )


def pick(stack, at):
    return lax.dynamic_index_in_dim(stack, at, 0, keepdims=False)


def place(stack, part, at):
    return lax.dynamic_update_slice_in_dim(stack, part[None], at % 4, 0)


def gather_near(block, leg, at):
    whole = jnp.zeros((4,) + block.shape, block.dtype)
    for shift in (0, 2, 3, 1):
        part = move(block, leg, shift) if shift else block
        whole = place(whole, part, at + 4 - shift)
    return whole


def scatter_near(stack, leg, at):
    total = pick(stack, at)
    for shift in (1, 3, 2):
        total += move(pick(stack, (at + shift) % 4).astype(bf16), leg, shift).astype(f32)
    return total


def cross(block, step):
    pairs = []
    for col in range(4):
        for x in range(4):
            pairs.append((col * 4 + x, col * 4 + ((x ^ 1) if (step + col) % 2 == 0 else 3 - x)))
    return lax.ppermute(block, ("col", "depth"), pairs)


def partner(at, core, step):
    return jnp.where((step + core) % 2 == 0, at ^ 1, 3 - at)


def turn_block(after_ref, *refs):
    blocks, out_ref = refs[:-1], refs[-1]
    for i, block in enumerate(blocks):

        @pl.when(pl.program_id(0) == i)
        def _(block=block):
            out_ref[...] = block[...].T


def turn(matrices, after):
    rows, columns = matrices[0].shape
    step = 256
    count = columns // step

    def at(i):
        return lambda m, j: (0, jnp.where(m == i, j, jnp.where(m < i, 0, count - 1)))

    return pl.pallas_call(
        turn_block,
        grid=(len(matrices), count),
        in_specs=[pl.BlockSpec(after.shape, lambda m, j: (0, 0))]
        + [pl.BlockSpec((rows, step), at(i)) for i in range(len(matrices))],
        out_specs=pl.BlockSpec((step, rows), lambda m, j: (m * count + j, 0)),
        out_shape=jax.ShapeDtypeStruct((len(matrices) * columns, rows), matrices[0].dtype),
        compiler_params=pltpu.CompilerParams(vmem_limit_bytes=24 * 2**20),
        cost_estimate=pl.CostEstimate(
            flops=0, bytes_accessed=4 * len(matrices) * rows * columns, transcendentals=0
        ),
    )(after, *matrices)


def hold_block(after_ref, block_ref, out_ref):
    out_ref[...] = block_ref[...]


def hold(matrix, after):
    rows, columns = matrix.shape
    step = 256
    return pl.pallas_call(
        hold_block,
        grid=(columns // step,),
        in_specs=[
            pl.BlockSpec(after.shape, lambda i: (0, 0)),
            pl.BlockSpec((rows, step), lambda i: (0, i)),
        ],
        out_specs=pl.BlockSpec((rows, step), lambda i: (0, i)),
        out_shape=jax.ShapeDtypeStruct(matrix.shape, matrix.dtype),
        compiler_params=pltpu.CompilerParams(vmem_limit_bytes=24 * 2**20),
        cost_estimate=pl.CostEstimate(
            flops=0, bytes_accessed=4 * rows * columns, transcendentals=0
        ),
    )(after, matrix)


def shards(tokens, w_up, grad_hidden):
    row, col, depth = lax.axis_index("row"), lax.axis_index("col"), lax.axis_index("depth")
    z, y, core = (row // 4) * 2 + col // 2, row % 4, col % 2
    first, second = jnp.where(core == 0, y, z), jnp.where(core == 0, z, y)
    share, width = tokens.shape
    hidden = w_up.shape[1]

    def slot(at):
        return jnp.where(core == 0, at % 4, (at % 2) * 2 + (at % 4) // 2)

    def side_order(rows):
        return jnp.where(core == 0, rows.swapaxes(0, 1), rows)

    w_other = swap(w_up)
    cotangent = grad_hidden.reshape(2, 2, 2, share, hidden)
    cotangent_other = swap(lax.dynamic_index_in_dim(cotangent, 1 - core, 2, keepdims=False))
    cotangent = lax.dynamic_index_in_dim(cotangent, core, 2, keepdims=False)

    line = gather_near(tokens, "first", first).reshape(-1, width)
    count = line.shape[0]
    half = count // 2
    below, above = move(line, "second", 1), move(line, "second", -1)
    held = hold(w_other, line[:16, :128])
    held, below, above = tie(held, below, above)
    beyond = jnp.concatenate(
        [move(below[:half], "second", 1), move(above[half:], "second", -1)], 0
    )
    every = jnp.zeros((2, 4) + line.shape, bf16)
    sums = [jnp.zeros((4, count, hidden), f32) for _ in range(2)]
    for shift, part in ((0, line), (3, below), (1, above), (2, beyond)):
        every = lax.dynamic_update_slice(every, part[None, None], (0, (second + shift) % 4, 0, 0))
        every = lax.dynamic_update_slice(
            every, swap(part)[None, None], (1, (first + shift) % 4, 0, 0)
        )
        for i, weight in enumerate((w_up, held)):
            product = jnp.dot(part, weight, preferred_element_type=f32)
            sums[i] = place(sums[i], product, second + shift)

    def split(total):
        rows = total.reshape(2, 2, 2, 2, share, hidden).transpose(0, 2, 1, 3, 4, 5)
        return rows.reshape(4, count, hidden)

    stack = jnp.concatenate([split(total) for total in sums], -1)
    near, mate = partner(depth, core, 0), partner(depth, core, 1)
    near_mate = partner(near, core, 1)
    away = jnp.stack([pick(stack, slot(near)), pick(stack, slot(near_mate))], 0).astype(bf16)
    got = cross(away, 0)
    send = (pick(stack, slot(mate)) + got[1].astype(f32)).astype(bf16)
    pre_act = pick(stack, slot(depth)) + got[0].astype(f32) + cross(send, 1).astype(f32)

    edge = lax.erf(pre_act * root_half)
    act = (0.5 * pre_act * (1.0 + edge)).astype(bf16).reshape(2, 2, share, 2 * hidden)
    slope = 0.5 * (1.0 + edge) + pre_act * norm_density * jnp.exp(-0.5 * pre_act * pre_act)
    cotangent = side_order(jnp.concatenate([cotangent, cotangent_other], -1))
    grad_own = (cotangent.reshape(pre_act.shape).astype(f32) * slope).astype(bf16)

    lower, upper = move(grad_own, "depth", 1), move(grad_own, "depth", -1)
    turned = turn((w_up, held), grad_own[:16, :128])
    turned, lower, upper = tie(turned, lower, upper)
    middle = count // 2
    opposite = jnp.concatenate(
        [move(lower[:middle], "depth", 1), move(upper[middle:], "depth", -1)], 0
    )
    grads = jnp.zeros((4,) + grad_own.shape, bf16)
    for shift, part in ((0, grad_own), (3, lower), (1, upper), (2, opposite)):
        grads = place(grads, part, slot(depth + shift))
    grads = grads.reshape(2, 2, 2, 2 * share, 2 * hidden)

    def piece_of(grads, shift):
        at = (second + shift) % 4
        return lax.dynamic_slice(
            grads, (at // 2, 0, at % 2, 0, 0), (1, 2, 1) + grads.shape[3:]
        ).reshape(count, 2 * hidden)

    far = jnp.dot(piece_of(grads, 2), turned, preferred_element_type=f32).astype(bf16)
    far, grads = tie(far, grads)
    low, high = move(far[:half], "second", 1), move(far[half:], "second", -1)
    rest = jnp.concatenate([piece_of(grads, shift) for shift in (1, 3, 0)], 0)
    rest = jnp.dot(rest, turned, preferred_element_type=f32)
    up, down, ours = rest[:count], rest[count : 2 * count], rest[2 * count :]
    up = jnp.concatenate([up[:half] + low.astype(f32), up[half:]], 0).astype(bf16)
    down = jnp.concatenate([down[:half], down[half:] + high.astype(f32)], 0).astype(bf16)

    order = grads.transpose(0, 2, 1, 3, 4).reshape(16 * share, 2 * hidden)
    beside = jnp.concatenate([order[:, :hidden], swap(order[:, hidden:])], 0)
    flat = every.reshape(-1, width)
    up, down, beside, flat = tie(up, down, beside, flat)
    from_below, from_above = move(up, "second", 1), move(down, "second", -1)
    weight_grad = lax.dot_general(
        flat, beside, (((0,), (0,)), ((), ())), preferred_element_type=f32
    ).astype(bf16)
    weight_grad, ours, from_below, from_above = tie(weight_grad, ours, from_below, from_above)
    ours = ours + from_below.astype(f32) + from_above.astype(f32)
    input_grad = scatter_near(ours.reshape(4, share, width), "first", first).astype(bf16)

    act_own, act_other = side_order(act[..., :hidden]), swap(side_order(act[..., hidden:]))
    hidden_act = jnp.stack(
        [jnp.where(core == 0, act_own, act_other), jnp.where(core == 0, act_other, act_own)], 2
    )
    return hidden_act.reshape(-1, hidden), input_grad, weight_grad


def tie(*values):
    return lax.optimization_barrier(values)


def solution(mesh):
    placed = (P(PLANE, "depth"), P("depth", PLANE), P("depth", PLANE))
    return jax.shard_map(
        shards,
        mesh=mesh,
        in_specs=placed,
        out_specs=(P("depth", PLANE), P(PLANE, "depth"), P("depth", PLANE)),
        check_vma=False,
    )
```

```python
import jax
import jax.numpy as jnp
from jax import lax
from jax.experimental import pallas as pl
from jax.experimental.pallas import tpu as pltpu
from jax.sharding import PartitionSpec as P

root_half = 0.7071067811865476
norm_density = 0.3989422804014327
PLANE = ("row", "col")
f32, bf16 = jnp.float32, jnp.bfloat16


def spot(z, y, core):
    return ((z // 2) * 4 + y) * 4 + (z % 2) * 2 + core


def plane_pairs(leg, way):
    pairs = []
    for z in range(4):
        for y in range(4):
            for core in range(2):
                on_y = (leg == "first") == (core == 0)
                to = ((z, (y + way) % 4) if on_y else ((z + way) % 4, y)) + (core,)
                pairs.append((spot(z, y, core), spot(*to)))
    return pairs


def move(block, leg, way):
    if leg == "depth":
        return lax.ppermute(block, "depth", [(i, (i + way) % 4) for i in range(4)])
    return lax.ppermute(block, PLANE, plane_pairs(leg, way))


def swap(block):
    return lax.ppermute(
        block,
        PLANE,
        [(spot(z, y, c), spot(z, y, 1 - c)) for z in range(4) for y in range(4) for c in range(2)],
    )


def pick(stack, at):
    return lax.dynamic_index_in_dim(stack, at, 0, keepdims=False)


def place(stack, part, at):
    return lax.dynamic_update_slice_in_dim(stack, part[None], at % 4, 0)


def gather_near(block, leg, at):
    whole = jnp.zeros((4,) + block.shape, block.dtype)
    for shift in (0, 2, 3, 1):
        part = move(block, leg, shift) if shift else block
        whole = place(whole, part, at + 4 - shift)
    return whole


def scatter_near(stack, leg, at):
    total = pick(stack, at)
    for shift in (1, 3, 2):
        total += move(pick(stack, (at + shift) % 4).astype(bf16), leg, shift).astype(f32)
    return total


def cross(block, step):
    pairs = []
    for col in range(4):
        for x in range(4):
            pairs.append((col * 4 + x, col * 4 + ((x ^ 1) if (step + col) % 2 == 0 else 3 - x)))
    return lax.ppermute(block, ("col", "depth"), pairs)


def partner(at, core, step):
    return jnp.where((step + core) % 2 == 0, at ^ 1, 3 - at)


def turn_block(after_ref, *refs):
    blocks, out_ref = refs[:-1], refs[-1]
    for i, block in enumerate(blocks):

        @pl.when(pl.program_id(0) == i)
        def _(block=block):
            out_ref[...] = block[...].T


def turn(matrices, after):
    rows, columns = matrices[0].shape
    step = 256
    count = columns // step

    def at(i):
        return lambda m, j: (0, jnp.where(m == i, j, jnp.where(m < i, 0, count - 1)))

    return pl.pallas_call(
        turn_block,
        grid=(len(matrices), count),
        in_specs=[pl.BlockSpec(after.shape, lambda m, j: (0, 0))]
        + [pl.BlockSpec((rows, step), at(i)) for i in range(len(matrices))],
        out_specs=pl.BlockSpec((step, rows), lambda m, j: (m * count + j, 0)),
        out_shape=jax.ShapeDtypeStruct((len(matrices) * columns, rows), matrices[0].dtype),
        compiler_params=pltpu.CompilerParams(vmem_limit_bytes=24 * 2**20),
        cost_estimate=pl.CostEstimate(
            flops=0, bytes_accessed=4 * len(matrices) * rows * columns, transcendentals=0
        ),
    )(after, *matrices)


def hold_block(after_ref, block_ref, out_ref):
    out_ref[...] = block_ref[...]


def hold(matrix, after):
    rows, columns = matrix.shape
    step = 256
    return pl.pallas_call(
        hold_block,
        grid=(columns // step,),
        in_specs=[
            pl.BlockSpec(after.shape, lambda i: (0, 0)),
            pl.BlockSpec((rows, step), lambda i: (0, i)),
        ],
        out_specs=pl.BlockSpec((rows, step), lambda i: (0, i)),
        out_shape=jax.ShapeDtypeStruct(matrix.shape, matrix.dtype),
        compiler_params=pltpu.CompilerParams(vmem_limit_bytes=24 * 2**20),
        cost_estimate=pl.CostEstimate(
            flops=0, bytes_accessed=4 * rows * columns, transcendentals=0
        ),
    )(after, matrix)


def shards(tokens, w_up, grad_hidden):
    row, col, depth = lax.axis_index("row"), lax.axis_index("col"), lax.axis_index("depth")
    z, y, core = (row // 4) * 2 + col // 2, row % 4, col % 2
    first, second = jnp.where(core == 0, y, z), jnp.where(core == 0, z, y)
    share, width = tokens.shape
    hidden = w_up.shape[1]

    def slot(at):
        return jnp.where(core == 0, at % 4, (at % 2) * 2 + (at % 4) // 2)

    def side_order(rows):
        return jnp.where(core == 0, rows.swapaxes(0, 1), rows)

    w_other = swap(w_up)
    cotangent = grad_hidden.reshape(2, 2, 2, share, hidden)
    cotangent_other = swap(lax.dynamic_index_in_dim(cotangent, 1 - core, 2, keepdims=False))
    cotangent = lax.dynamic_index_in_dim(cotangent, core, 2, keepdims=False)

    line = gather_near(tokens, "first", first).reshape(-1, width)
    count = line.shape[0]
    half = count // 2
    below, above = move(line, "second", 1), move(line, "second", -1)
    held = hold(w_other, line[:16, :128])
    held, below, above = tie(held, below, above)
    beyond = jnp.concatenate(
        [move(below[:half], "second", 1), move(above[half:], "second", -1)], 0
    )
    every = jnp.zeros((2, 4) + line.shape, bf16)
    sums = [jnp.zeros((4, count, hidden), f32) for _ in range(2)]
    for shift, part in ((0, line), (3, below), (1, above), (2, beyond)):
        every = lax.dynamic_update_slice(every, part[None, None], (0, (second + shift) % 4, 0, 0))
        every = lax.dynamic_update_slice(
            every, swap(part)[None, None], (1, (first + shift) % 4, 0, 0)
        )
        for i, weight in enumerate((w_up, held)):
            product = jnp.dot(part, weight, preferred_element_type=f32)
            sums[i] = place(sums[i], product, second + shift)

    def split(total):
        rows = total.reshape(2, 2, 2, 2, share, hidden).transpose(0, 2, 1, 3, 4, 5)
        return rows.reshape(4, count, hidden)

    stack = jnp.concatenate([split(total) for total in sums], -1)
    near, mate = partner(depth, core, 0), partner(depth, core, 1)
    near_mate = partner(near, core, 1)
    away = jnp.stack([pick(stack, slot(near)), pick(stack, slot(near_mate))], 0).astype(bf16)
    got = cross(away, 0)
    send = (pick(stack, slot(mate)) + got[1].astype(f32)).astype(bf16)
    pre_act = pick(stack, slot(depth)) + got[0].astype(f32) + cross(send, 1).astype(f32)

    edge = lax.erf(pre_act * root_half)
    act = (0.5 * pre_act * (1.0 + edge)).astype(bf16).reshape(2, 2, share, 2 * hidden)
    slope = 0.5 * (1.0 + edge) + pre_act * norm_density * jnp.exp(-0.5 * pre_act * pre_act)
    cotangent = side_order(jnp.concatenate([cotangent, cotangent_other], -1))
    grad_own = (cotangent.reshape(pre_act.shape).astype(f32) * slope).astype(bf16)

    lower, upper = move(grad_own, "depth", 1), move(grad_own, "depth", -1)
    turned = turn((w_up, held), grad_own[:16, :128])
    turned, lower, upper = tie(turned, lower, upper)
    middle = count // 2
    opposite = jnp.concatenate(
        [move(lower[:middle], "depth", 1), move(upper[middle:], "depth", -1)], 0
    )
    grads = jnp.zeros((4,) + grad_own.shape, bf16)
    for shift, part in ((0, grad_own), (3, lower), (1, upper), (2, opposite)):
        grads = place(grads, part, slot(depth + shift))
    grads = grads.reshape(2, 2, 2, 2 * share, 2 * hidden)

    def piece_of(grads, shift):
        at = (second + shift) % 4
        return lax.dynamic_slice(
            grads, (at // 2, 0, at % 2, 0, 0), (1, 2, 1) + grads.shape[3:]
        ).reshape(count, 2 * hidden)

    far = jnp.dot(piece_of(grads, 2), turned, preferred_element_type=f32).astype(bf16)
    far, grads = tie(far, grads)
    low, high = move(far[:half], "second", 1), move(far[half:], "second", -1)
    rest = jnp.concatenate([piece_of(grads, shift) for shift in (1, 3)], 0)
    rest = jnp.dot(rest, turned, preferred_element_type=f32)
    up, down = rest[:count], rest[count:]
    up = jnp.concatenate([up[:half] + low.astype(f32), up[half:]], 0).astype(bf16)
    down = jnp.concatenate([down[:half], down[half:] + high.astype(f32)], 0).astype(bf16)

    order = grads.transpose(0, 2, 1, 3, 4).reshape(16 * share, 2 * hidden)
    beside = jnp.concatenate([order[:, :hidden], swap(order[:, hidden:])], 0)
    flat = every.reshape(-1, width)
    up, down, beside, flat, grads = tie(up, down, beside, flat, grads)
    from_below, from_above = move(up, "second", 1), move(down, "second", -1)
    ours = jnp.dot(piece_of(grads, 0), turned, preferred_element_type=f32)
    ours, beside = tie(ours, beside)
    weight_grad = lax.dot_general(
        flat, beside, (((0,), (0,)), ((), ())), preferred_element_type=f32
    ).astype(bf16)
    weight_grad, ours, from_below, from_above = tie(weight_grad, ours, from_below, from_above)
    ours = ours + from_below.astype(f32) + from_above.astype(f32)
    input_grad = scatter_near(ours.reshape(4, share, width), "first", first).astype(bf16)

    act_own, act_other = side_order(act[..., :hidden]), swap(side_order(act[..., hidden:]))
    hidden_act = jnp.stack(
        [jnp.where(core == 0, act_own, act_other), jnp.where(core == 0, act_other, act_own)], 2
    )
    return hidden_act.reshape(-1, hidden), input_grad, weight_grad


def tie(*values):
    return lax.optimization_barrier(values)


def solution(mesh):
    placed = (P(PLANE, "depth"), P("depth", PLANE), P("depth", PLANE))
    return jax.shard_map(
        shards,
        mesh=mesh,
        in_specs=placed,
        out_specs=(P("depth", PLANE), P(PLANE, "depth"), P("depth", PLANE)),
        check_vma=False,
    )
```
